32 devices in a mesh: hyp: 8 (over y, x, core), head: 4 (over z).
Axes of the slice: x: 2, y: 2, z: 4, core: 2. Of those that a mesh axis runs over, the one named last changes fastest.
Arguments:
- step_embeds: bfloat16 [3, 128, 4096], P(None, 'hyp'), may hold values from -6 to 6
- lang_table: bfloat16 [8, 4096], replicated, may hold values from -3 to 3
- lang_ids: int32 [8, 4], replicated, may hold values from 0 to 7
- self_gain: float32 [4096], replicated, may hold values from 0.1 to 1.9
- self_wq: bfloat16 [4096, 2048], P(None, 'head'), may hold values from -0.09375 to 0.09375
- self_wk: bfloat16 [4096, 2048], P(None, 'head'), may hold values from -0.09375 to 0.09375
- self_wv: bfloat16 [4096, 2048], P(None, 'head'), may hold values from -0.09375 to 0.09375
- self_wo: bfloat16 [2048, 4096], P('head'), may hold values from -0.125 to 0.125
- cross_gain: float32 [4096], replicated, may hold values from 0.1 to 1.9
- cross_wq: bfloat16 [4096, 2048], P(None, 'head'), may hold values from -0.09375 to 0.09375
- cross_wkv: bfloat16 [4096, 4096], P('hyp', 'head'), may hold values from -0.09375 to 0.09375
- encoder_rows: bfloat16 [6144, 4096], P('hyp', 'head'), may hold values from -200 to 200
- doc_lengths: int32 [8], P('hyp'), may hold values from 192 to 768, as said below
- past_keys: bfloat16 [128, 32, 2048], P('hyp', None, 'head'), may hold values from -200 to 200
- past_values: bfloat16 [128, 32, 2048], P('hyp', None, 'head'), may hold values from -6 to 6
- parents: int32 [3, 128], replicated, may hold values from 0 to 3
Outputs:
- cross_context: bfloat16 [3, 128, 2048], P(None, 'hyp', 'head')
- final_keys: bfloat16 [128, 35, 2048], P('hyp', None, 'head')
- final_values: bfloat16 [128, 35, 2048], P('hyp', None, 'head')
The draws below stay inside these ranges and needn't reach their ends.
Inputs may be any that keep to these rules, and one draw needn't show every extreme that they name: `doc_lengths`: some document has exactly 768 live rows. `parents`: A parent is a beam of the same document and target.
All inputs are finite; a program needn't handle non-finite values.
Results may differ from the reference program's by a relative error of at most 0.03.
Values may be sent and summed in bfloat16 or wider, within the bound.
A program may use at most 128 MiB of HBM per device.

```python
import jax
import jax.numpy as jnp
from jax import lax

D = 4096
HEADS = 8
HEAD = 256
BEAMS = 4
TARGETS = 4
LEN = 768
STEPS = 3
LANGS = 8
PAST = 32
DOCS = 8
HYPS = 128


def spiked_rows(key, row_total, col_total):
    base = jnp.clip(jax.random.normal(key, (row_total, col_total), jnp.float32), -4.0, 4.0)
    return base


def scaled_rows(key, row_total, col_total):
    base = jnp.clip(jax.random.normal(key, (row_total, col_total), jnp.float32), -4.0, 4.0)
    return base


def draw_encoder_rows(key, part):
    return scaled_rows(jax.random.fold_in(key, 3), DOCS * LEN, D).astype(jnp.bfloat16)


def draw_past_keys(key, part):
    flat = spiked_rows(jax.random.fold_in(key, 4), HYPS * PAST, HEADS * HEAD)
    return flat.reshape(HYPS, PAST, HEADS * HEAD).astype(jnp.bfloat16)


def draw_doc_lengths(key, part):
    lengths = jax.random.randint(jax.random.fold_in(key, 1), (DOCS,), LEN // 4, LEN + 1, jnp.int32)
    longest = jax.random.randint(jax.random.fold_in(key, 2), (), 0, DOCS, jnp.int32)
    return lengths.at[longest].set(LEN)


def place_ends(array, stream_key, low, largest):
    longest = array.shape.index(max(array.shape))
    spots = []
    for shift in (0, 1):
        where = [jax.random.randint(jax.random.fold_in(stream_key, axis), (), 0, length) for axis, length in enumerate(array.shape)]
        where[longest] = (where[longest] + shift) % array.shape[longest]
        spots.append(tuple(where))
    return array.at[spots[0]].set(low).at[spots[1]].set(largest)


def levels(own_key, shape, cuts, smallest, top_value):
    def one(position, parts):
        heights = jax.random.uniform(jax.random.fold_in(jax.random.fold_in(own_key, 6), position), (parts,), jnp.float32, smallest / len(cuts), top_value / len(cuts))
        return jnp.repeat(jnp.exp(heights), shape[position] // parts).reshape((-1,) + (1,) * (len(shape) - position - 1))

    level = one(*cuts[0])
    for cut in cuts[1:]:
        level = level * one(*cut)
    return level


def gaussian(own_key, shape, scale, reach, split=(), kind=jnp.bfloat16):
    values = jax.random.normal(own_key, shape, jnp.float32) * scale
    if len(split) > 0:
        values = levels(own_key, shape, split, -0.22, 0.18) * values
    return jnp.clip(values, min=-reach, max=reach).astype(kind)


def setup_inputs(seed: int = 0) -> dict:
    keys = jax.random.split(jax.random.key(seed), 17)
    return {
        "step_embeds": gaussian(keys[0], (STEPS, HYPS, D), 1.0, 6.0, ((1, 8),)),
        "lang_table": gaussian(keys[1], (LANGS, D), 0.5, 3.0),
        "lang_ids": place_ends(jax.random.randint(keys[2], (DOCS, TARGETS), 0, LANGS), jax.random.fold_in(keys[2], 1), 0, LANGS - 1).astype(jnp.int32),
        "self_gain": jnp.clip(1.0 + 0.18 * jax.random.normal(keys[3], (D,), jnp.float32), 0.1, 1.9),
        "self_wq": gaussian(keys[4], (D, HEADS * HEAD), D ** -0.5, 0.09375, ((1, 4),)),
        "self_wk": gaussian(keys[5], (D, HEADS * HEAD), D ** -0.5, 0.09375, ((1, 4),)),
        "self_wv": gaussian(keys[6], (D, HEADS * HEAD), D ** -0.5, 0.09375, ((1, 4),)),
        "self_wo": gaussian(keys[7], (HEADS * HEAD, D), (HEADS * HEAD) ** -0.5, 0.125, ((0, 4),)),
        "cross_gain": jnp.clip(1.0 + 0.18 * jax.random.normal(keys[8], (D,), jnp.float32), 0.1, 1.9),
        "cross_wq": gaussian(keys[9], (D, HEADS * HEAD), D ** -0.5, 0.09375, ((1, 4),)),
        "cross_wkv": gaussian(keys[10], (D, 2 * HEADS * HEAD), D ** -0.5, 0.09375, ((0, 8), (1, 4))),
        "encoder_rows": draw_encoder_rows(jax.random.fold_in(keys[16], 71), 0),
        "doc_lengths": draw_doc_lengths(jax.random.fold_in(keys[16], 71), 0),
        "past_keys": draw_past_keys(jax.random.fold_in(keys[16], 71), 0),
        "past_values": gaussian(keys[14], (HYPS, PAST, HEADS * HEAD), 1.0, 6.0, ((0, 8), (2, 4))),
        "parents": place_ends(jax.random.randint(keys[15], (STEPS, HYPS), 0, BEAMS), jax.random.fold_in(keys[15], 1), 0, BEAMS - 1).astype(jnp.int32),
    }


EPSILON = 1e-06

def rms_scaled(values_in, gain):
    mean_square = lax.optimization_barrier(jnp.mean(values_in * values_in, axis=-1, keepdims=True))
    return values_in * lax.rsqrt(mean_square + EPSILON) * gain

def cross_attend(inputs):
    queries, cross_keys, cross_values, doc_length = inputs
    scaling = HEAD ** (-0.5)
    scores = jnp.einsum('qhd,jhd->hqj', queries.astype(jnp.float32), cross_keys.astype(jnp.float32)) * scaling
    live_mask = jnp.arange(LEN, dtype=jnp.int32) < doc_length
    scores = jnp.where(live_mask[None, None, :], scores, -jnp.inf)
    highest = lax.optimization_barrier(jnp.max(scores, axis=2, keepdims=True))
    raw_weights = jnp.exp(scores - highest)
    totals = lax.optimization_barrier(jnp.sum(raw_weights, axis=2, keepdims=True))
    weights = (raw_weights / totals).astype(jnp.bfloat16)
    output = jnp.einsum('hqj,jhd->qhd', weights.astype(jnp.float32), cross_values.astype(jnp.float32))
    return output.astype(jnp.bfloat16)

def reference(step_embeds, lang_table, lang_ids, self_gain, self_wq, self_wk, self_wv, self_wo, cross_gain, cross_wq, cross_wkv, encoder_rows, doc_lengths, past_keys, past_values, parents):
    hyp_ids = jnp.arange(HYPS, dtype=jnp.int32)
    doc_of = hyp_ids // TARGETS % DOCS
    target_of = hyp_ids % TARGETS
    lang_rows = lang_table[lang_ids[doc_of, target_of]].astype(jnp.float32)

    def project(doc_rows):
        return jnp.dot(doc_rows, cross_wkv, preferred_element_type=jnp.float32).astype(jnp.bfloat16)
    cross_kv = lax.map(project, encoder_rows.reshape(DOCS, LEN, D)).reshape(DOCS, LEN, HEADS, 2, HEAD)
    cross_keys = cross_kv[:, :, :, 0, :]
    cross_values = cross_kv[:, :, :, 1, :]
    cache_keys, cache_values = (past_keys, past_values)
    scaling = HEAD ** (-0.5)
    contexts = []
    for step_idx in range(STEPS):
        source = (parents[step_idx] * DOCS + doc_of) * TARGETS + target_of
        cache_keys = cache_keys[source]
        cache_values = cache_values[source]
        hidden_in = step_embeds[step_idx].astype(jnp.float32) + lang_rows
        normed = rms_scaled(hidden_in, self_gain).astype(jnp.bfloat16)
        new_query = jnp.dot(normed, self_wq, preferred_element_type=jnp.float32).astype(jnp.bfloat16)
        new_key = jnp.dot(normed, self_wk, preferred_element_type=jnp.float32).astype(jnp.bfloat16)
        new_value = jnp.dot(normed, self_wv, preferred_element_type=jnp.float32).astype(jnp.bfloat16)
        cache_keys = jnp.concatenate([cache_keys, new_key[:, None, :]], axis=1)
        cache_values = jnp.concatenate([cache_values, new_value[:, None, :]], axis=1)
        query_f = new_query.astype(jnp.float32).reshape(HYPS, HEADS, HEAD)
        key_f = cache_keys.astype(jnp.float32).reshape(HYPS, -1, HEADS, HEAD)
        value_f = cache_values.astype(jnp.float32).reshape(HYPS, -1, HEADS, HEAD)
        scores = jnp.einsum('rhd,rphd->rhp', query_f, key_f) * scaling
        highest = lax.optimization_barrier(jnp.max(scores, axis=2, keepdims=True))
        raw_weights = jnp.exp(scores - highest)
        totals = lax.optimization_barrier(jnp.sum(raw_weights, axis=2))
        summed = jnp.einsum('rhp,rphd->rhd', raw_weights, value_f)
        self_context = (summed / totals[:, :, None]).reshape(HYPS, HEADS * HEAD).astype(jnp.bfloat16)
        residual = hidden_in + jnp.dot(self_context, self_wo, preferred_element_type=jnp.float32)
        normed_cross = rms_scaled(residual, cross_gain).astype(jnp.bfloat16)
        cross_query = jnp.dot(normed_cross, cross_wq, preferred_element_type=jnp.float32).astype(jnp.bfloat16)
        grouped = cross_query.reshape(BEAMS, DOCS, TARGETS, HEADS, HEAD).transpose(1, 0, 2, 3, 4).reshape(DOCS, BEAMS * TARGETS, HEADS, HEAD)
        attended = lax.map(cross_attend, (grouped, cross_keys, cross_values, doc_lengths))
        restored = attended.reshape(DOCS, BEAMS, TARGETS, HEADS * HEAD).transpose(1, 0, 2, 3).reshape(HYPS, HEADS * HEAD)
        contexts.append(restored)
    return (jnp.stack(contexts), cache_keys, cache_values)
```

```python
import jax
import jax.numpy as jnp
from jax import lax
from jax.sharding import PartitionSpec as P

HEAD = 256
BEAMS = 4
STEPS = 3
EPSILON = 1e-06


def rms_scaled(values_in, gain):
    mean_square = jnp.mean(values_in * values_in, axis=-1, keepdims=True)
    return values_in * lax.rsqrt(mean_square + EPSILON) * gain


def pick(candidates, selector):
    chosen = candidates[0]
    shape = selector.shape + (1,) * (chosen.ndim - selector.ndim)
    for position in range(1, len(candidates)):
        chosen = jnp.where((selector == position).reshape(shape), candidates[position], chosen)
    return chosen


def choose(flags, first, second):
    return jnp.where(flags.reshape(flags.shape + (1,) * (first.ndim - flags.ndim)), first, second)


def compose(outer, inner):
    return pick([jnp.broadcast_to(outer[b][None], inner.shape) for b in range(BEAMS)], inner)


def swap(block, bit, group_size):
    count = lax.axis_size("hyp")
    route = [(i, ((i // group_size) ^ bit) * group_size + i % group_size) for i in range(count)]
    return lax.ppermute(block, "hyp", route)


def final_cache(past, bit, my_beam, ancestors, group_size):
    other = 3 - bit
    mate = swap(past, bit, group_size)
    mine_set = (my_beam & bit) != 0
    low = jnp.where(mine_set, mate, past)
    high = jnp.where(mine_set, past, mate)
    peer_rows = lax.dynamic_index_in_dim(ancestors, my_beam ^ other, 0, keepdims=False)
    my_rows = lax.dynamic_index_in_dim(ancestors, my_beam, 0, keepdims=False)
    arrived = swap(choose((peer_rows & bit) != 0, high, low), other, group_size)
    local = choose((my_rows & bit) != 0, high, low)
    return choose((my_rows & other) == (my_beam & other), local, arrived)


def cross_attend(queries, cross_keys, cross_values, doc_length):
    query_rows = queries.shape[0]
    heads_here = cross_keys.shape[1]
    scores = jnp.einsum(
        "qhd,jhd->hqj",
        queries.reshape(query_rows, heads_here, HEAD),
        cross_keys,
        preferred_element_type=jnp.float32,
    ) * (HEAD ** (-0.5))
    live_mask = lax.broadcasted_iota(jnp.int32, (1, 1, cross_keys.shape[0]), 2) < doc_length
    scores = jnp.where(live_mask, scores, -jnp.inf)
    highest = jnp.max(scores, axis=2, keepdims=True)
    raw_weights = jnp.exp(scores - highest)
    totals = jnp.sum(raw_weights, axis=2, keepdims=True)
    weights = (raw_weights / totals).astype(jnp.bfloat16)
    output = jnp.einsum("hqj,jhd->qhd", weights, cross_values, preferred_element_type=jnp.float32)
    return output.reshape(query_rows, heads_here * HEAD).astype(jnp.bfloat16)


def project_rows(encoder_rows, cross_wkv):
    size = lax.axis_size("head")
    me = lax.axis_index("head")
    width = encoder_rows.shape[1]
    full_weights = lax.all_gather(cross_wkv, "hyp", axis=0, tiled=True)

    def term(rows, owner):
        owner = jnp.clip(owner, 0, size - 1)
        weights = lax.dynamic_slice_in_dim(full_weights, owner * width, width, 0)
        return jnp.dot(rows, weights, preferred_element_type=jnp.float32)

    upward = [(i, i + 1) for i in range(size - 1)]
    downward = [(i + 1, i) for i in range(size - 1)]
    up = down = encoder_rows
    total = term(encoder_rows, me)
    for step in range(1, size):
        up = lax.ppermute(up, "head", upward)
        down = lax.ppermute(down, "head", downward)
        total = total + term(up, me - step)
        total = total + term(down, me + step)
        upward, downward = upward[1:], downward[:-1]
    return total.astype(jnp.bfloat16)


def shards(
    step_embeds,
    lang_table,
    lang_ids,
    self_gain,
    self_wq,
    self_wk,
    self_wv,
    self_wo,
    cross_gain,
    cross_wq,
    cross_wkv,
    encoder_rows,
    doc_lengths,
    past_keys,
    past_values,
    parents,
):
    hyp_count = lax.axis_size("hyp")
    head_parts = lax.axis_size("head")
    group_size = hyp_count // BEAMS
    my_index = lax.axis_index("hyp")
    my_beam = my_index // group_size
    my_slot = my_index % group_size
    rows = step_embeds.shape[1]
    features = step_embeds.shape[2]
    head_width = self_wq.shape[1]
    heads = head_width // HEAD
    past = past_keys.shape[1]
    docs_here = lang_ids.shape[0] // group_size
    targets = lang_ids.shape[1]
    scaling = HEAD ** (-0.5)
    beam_groups = [[b * group_size + s for b in range(BEAMS)] for s in range(group_size)]

    cross_kv = project_rows(encoder_rows, cross_wkv)
    cross_kv = cross_kv.reshape(encoder_rows.shape[0], heads, 2, HEAD)

    my_langs = lax.dynamic_slice_in_dim(lang_ids, my_slot * docs_here, docs_here, 0).reshape(rows)
    one_hot = (
        my_langs[:, None] == lax.broadcasted_iota(jnp.int32, (1, lang_table.shape[0]), 1)
    ).astype(jnp.bfloat16)
    lang_rows = jnp.dot(one_hot, lang_table, preferred_element_type=jnp.float32)
    hidden_in = (step_embeds.astype(jnp.float32) + lang_rows[None]).reshape(STEPS * rows, features)
    normed = rms_scaled(hidden_in, self_gain).astype(jnp.bfloat16)
    made = [
        jnp.dot(normed, w, preferred_element_type=jnp.float32).astype(jnp.bfloat16)
        for w in (self_wq, self_wk, self_wv)
    ]
    every = lax.all_gather(
        jnp.concatenate(made, axis=1), "hyp", axis=0, tiled=False, axis_index_groups=beam_groups
    ).reshape(BEAMS, STEPS, rows, 3, head_width)
    queries, keys, values = every[:, :, :, 0], every[:, :, :, 1], every[:, :, :, 2]

    parent_view = parents.reshape(STEPS, BEAMS, -1)
    moves = lax.dynamic_slice_in_dim(parent_view, my_slot * rows, rows, 2)
    ancestors = []
    for s in range(STEPS):
        chain = {s: None}
        current = moves[s]
        for j in range(s - 1, -2, -1):
            chain[j] = current
            if j >= 0:
                current = compose(moves[j], current)
        ancestors.append(chain)

    def of_mine(table):
        return lax.dynamic_index_in_dim(table, my_beam, 0, keepdims=False)

    past_k = past_keys.reshape(rows, past, heads, HEAD)
    past_v = past_values.reshape(rows, past, heads, HEAD)
    split_q = queries.reshape(BEAMS * STEPS, rows, heads, HEAD)
    scores = (
        jnp.einsum("nrhd,rphd->rhnp", split_q, past_k, preferred_element_type=jnp.float32)
        * scaling
    )
    highest = jnp.max(scores, axis=3)
    weights = jnp.exp(scores - highest[..., None])
    totals = jnp.sum(weights, axis=3)
    summed = jnp.einsum("rhnp,rphd->nrhd", weights, past_v.astype(jnp.float32))
    stats = jnp.stack([highest, totals], axis=-1).transpose(2, 0, 1, 3)
    packed = jnp.concatenate(
        [
            summed.reshape(BEAMS, STEPS * rows, head_width),
            stats.reshape(BEAMS, STEPS * rows, heads * 2),
        ],
        axis=2,
    )
    returned = lax.all_to_all(
        packed, "hyp", 0, 0, tiled=True, axis_index_groups=beam_groups
    ).reshape(BEAMS, STEPS, rows, head_width + heads * 2)
    past_of = jnp.stack([of_mine(ancestors[s][-1]) for s in range(STEPS)])
    chosen = pick([returned[b] for b in range(BEAMS)], past_of)
    part_sum = chosen[..., :head_width].reshape(STEPS, rows, heads, HEAD)
    part_stats = chosen[..., head_width:].reshape(STEPS, rows, heads, 2)

    contexts = []
    last_keys, last_values = [], []
    for s in range(STEPS):
        my_query = of_mine(queries[:, s]).reshape(rows, heads, HEAD).astype(jnp.float32)
        high, added, score_list, value_list = part_stats[s, ..., 0], None, [], []
        for j in range(s + 1):
            if j == s:
                key, value = of_mine(keys[:, j]), of_mine(values[:, j])
            else:
                owner = of_mine(ancestors[s][j])
                key = pick([keys[b, j] for b in range(BEAMS)], owner)
                value = pick([values[b, j] for b in range(BEAMS)], owner)
            if s == STEPS - 1:
                last_keys.append(key)
                last_values.append(value)
            key = key.reshape(rows, heads, HEAD).astype(jnp.float32)
            score_list.append(jnp.sum(my_query * key, axis=-1) * scaling)
            value_list.append(value.reshape(rows, heads, HEAD).astype(jnp.float32))
        top = high
        for score in score_list:
            top = jnp.maximum(top, score)
        factor = jnp.exp(high - top)
        total = part_stats[s, ..., 1] * factor
        context = part_sum[s] * factor[..., None]
        for score, value in zip(score_list, value_list):
            weight = jnp.exp(score - top)
            total = total + weight
            context = context + weight[..., None] * value
        contexts.append((context / total[..., None]).reshape(rows, head_width))
    self_context = jnp.concatenate(contexts, axis=0).astype(jnp.bfloat16)

    partial_out = jnp.dot(self_context, self_wo, preferred_element_type=jnp.float32).astype(
        jnp.bfloat16
    )
    share = features // head_parts
    spread = lax.all_to_all(
        partial_out.reshape(STEPS * rows, head_parts, share).transpose(1, 0, 2),
        "head", 0, 0, tiled=True,
    )
    own_sum = jnp.sum(spread.astype(jnp.float32), axis=0).astype(jnp.bfloat16)
    full_sum = lax.all_gather(own_sum, "head", axis=1, tiled=True)
    residual = hidden_in + full_sum.astype(jnp.float32)
    normed_cross = rms_scaled(residual, cross_gain).astype(jnp.bfloat16)
    cross_query = jnp.dot(normed_cross, cross_wq, preferred_element_type=jnp.float32).astype(
        jnp.bfloat16
    )

    by_doc = cross_query.reshape(STEPS, docs_here, targets, head_width).transpose(1, 0, 2, 3)
    by_doc = by_doc.reshape(1, docs_here, STEPS * targets, head_width)
    slots = jnp.arange(group_size)
    outgoing = jnp.where(
        (slots == my_slot)[:, None, None, None], by_doc, jnp.zeros((), by_doc.dtype)
    ).reshape(hyp_count, STEPS * targets, head_width)
    incoming = lax.all_to_all(outgoing, "hyp", 0, 0, tiled=True)
    source_slot = my_index // docs_here
    doc_queries = lax.dynamic_index_in_dim(
        incoming.reshape(BEAMS, group_size, STEPS * targets, head_width), source_slot, 1, False
    ).reshape(BEAMS * STEPS * targets, head_width)
    answer = cross_attend(doc_queries, cross_kv[:, :, 0, :], cross_kv[:, :, 1, :], doc_lengths[0])

    by_beam = answer.reshape(BEAMS, 1, STEPS * targets, head_width)
    outgoing = jnp.where(
        (slots == source_slot)[None, :, None, None], by_beam, jnp.zeros((), by_beam.dtype)
    ).reshape(hyp_count, STEPS * targets, head_width)
    incoming = lax.all_to_all(outgoing, "hyp", 0, 0, tiled=True)
    mine = lax.dynamic_slice_in_dim(incoming, my_slot * docs_here, docs_here, 0)
    cross_context = (
        mine.reshape(docs_here, STEPS, targets, head_width)
        .transpose(1, 0, 2, 3)
        .reshape(STEPS, rows, head_width)
    )

    last = ancestors[STEPS - 1][-1]
    out_keys = final_cache(past_keys, 1, my_beam, last, group_size)
    out_values = final_cache(past_values, 2, my_beam, last, group_size)
    final_keys = jnp.concatenate([out_keys, jnp.stack(last_keys, axis=1)], axis=1)
    final_values = jnp.concatenate([out_values, jnp.stack(last_values, axis=1)], axis=1)
    return (cross_context, final_keys, final_values)


def solution(mesh):
    return jax.shard_map(
        shards,
        mesh=mesh,
        in_specs=(
            P(None, "hyp", None),
            P(),
            P(),
            P(),
            P(None, "head"),
            P(None, "head"),
            P(None, "head"),
            P("head", None),
            P(),
            P(None, "head"),
            P("hyp", "head"),
            P("hyp", "head"),
            P("hyp"),
            P("hyp", None, "head"),
            P("hyp", None, "head"),
            P(),
        ),
        out_specs=(P(None, "hyp", "head"), P("hyp", None, "head"), P("hyp", None, "head")),
        check_vma=False,
    )
```

```python
import functools

import jax
import jax.numpy as jnp
from jax import lax
from jax.experimental import pallas as pl
from jax.experimental.pallas import tpu as pltpu
from jax.sharding import PartitionSpec as P

HEAD = 256
BEAMS = 4
STEPS = 3
EPSILON = 1e-06


def rms_scaled(values_in, gain):
    mean_square = jnp.mean(values_in * values_in, axis=-1, keepdims=True)
    return values_in * lax.rsqrt(mean_square + EPSILON) * gain


def pick(candidates, selector):
    chosen = candidates[0]
    shape = selector.shape + (1,) * (chosen.ndim - selector.ndim)
    for position in range(1, len(candidates)):
        chosen = jnp.where((selector == position).reshape(shape), candidates[position], chosen)
    return chosen


def choose(flags, first, second):
    return jnp.where(flags.reshape(flags.shape + (1,) * (first.ndim - flags.ndim)), first, second)


def compose(outer, inner):
    return pick([jnp.broadcast_to(outer[b][None], inner.shape) for b in range(BEAMS)], inner)


def swap(block, bit, group_size):
    count = lax.axis_size("hyp")
    route = [(i, ((i // group_size) ^ bit) * group_size + i % group_size) for i in range(count)]
    return lax.ppermute(block, "hyp", route)


def final_cache(past, bit, my_beam, ancestors, group_size):
    other = 3 - bit
    mate = swap(past, bit, group_size)
    mine_set = (my_beam & bit) != 0
    low = jnp.where(mine_set, mate, past)
    high = jnp.where(mine_set, past, mate)
    peer_rows = lax.dynamic_index_in_dim(ancestors, my_beam ^ other, 0, keepdims=False)
    my_rows = lax.dynamic_index_in_dim(ancestors, my_beam, 0, keepdims=False)
    arrived = swap(choose((peer_rows & bit) != 0, high, low), other, group_size)
    local = choose((my_rows & bit) != 0, high, low)
    return choose((my_rows & other) == (my_beam & other), local, arrived)


def cross_attend(queries, cross_kv, doc_length):
    rows = cross_kv.shape[0]
    live_mask = lax.broadcasted_iota(jnp.int32, (1, rows), 1) < doc_length
    outputs = []
    for head in range(queries.shape[1] // HEAD):
        query = queries[:, head * HEAD : (head + 1) * HEAD]
        keys = cross_kv[:, 2 * head * HEAD : (2 * head + 1) * HEAD]
        values = cross_kv[:, (2 * head + 1) * HEAD : (2 * head + 2) * HEAD]
        scores = lax.dot_general(
            query, keys, (((1,), (1,)), ((), ())), preferred_element_type=jnp.float32
        ) * (HEAD ** (-0.5))
        scores = jnp.where(live_mask, scores, -jnp.inf)
        raw_weights = jnp.exp(scores - jnp.max(scores, axis=1, keepdims=True))
        totals = jnp.sum(raw_weights, axis=1, keepdims=True)
        weights = (raw_weights / totals).astype(jnp.bfloat16)
        outputs.append(jnp.dot(weights, values, preferred_element_type=jnp.float32))
    return jnp.concatenate(outputs, axis=1).astype(jnp.bfloat16)


def gather_weights(block):
    size = lax.axis_size("hyp")
    me = lax.axis_index("hyp")
    blocks = block[None]
    bits = [1 << k for k in range(1, size.bit_length() - 1)] + [1]
    done = 0
    for bit in bits:
        arrived = lax.ppermute(blocks, "hyp", [(i, i ^ bit) for i in range(size)])
        mine_high = (me & bit) != 0
        low = jnp.where(mine_high, arrived, blocks)
        high = jnp.where(mine_high, blocks, arrived)
        if bit > done:
            blocks = jnp.concatenate([low, high], axis=0)
        else:
            blocks = jnp.stack([low, high], axis=1).reshape((-1,) + block.shape)
        done = max(done, bit)
    return blocks.reshape(size * block.shape[0], block.shape[1])


def project_rows(encoder_rows, cross_wkv):
    half = encoder_rows.shape[0] // 2
    parts = [
        lax.all_gather(encoder_rows[k * half : (k + 1) * half], "head", axis=1, tiled=True)
        for k in range(2)
    ]
    full_weights = gather_weights(cross_wkv)
    return jnp.concatenate(
        [
            jnp.dot(part, full_weights, preferred_element_type=jnp.float32).astype(jnp.bfloat16)
            for part in parts
        ],
        axis=0,
    )


def cross_query_kernel(
    docs_here, context, wo, hidden, gain, wq, arrived,
    part, landed, full, query, sum_send, sum_recv, all_send, all_recv, out_send, out_recv,
):
    size = lax.axis_size("head")
    me = lax.axis_index("head")
    hyps = lax.axis_size("hyp")
    group = hyps // BEAMS
    index = lax.axis_index("hyp")
    slot = lax.rem(index, group)
    beam = index // group
    share = part.shape[2]
    targets = [slot * docs_here + k for k in range(docs_here)]
    sources = [b * group + index // docs_here for b in range(BEAMS)]

    barrier = pltpu.get_barrier_semaphore()
    for d in range(1, size):
        pl.semaphore_signal(
            barrier, 1, device_id=(index, lax.rem(me + d, size)), device_id_type=pl.DeviceIdType.MESH
        )
    expected = jnp.int32(size - 1)
    for peer in targets + sources:
        expected = expected + (peer != index).astype(jnp.int32)

        @pl.when(peer != index)
        def _():
            pl.semaphore_signal(
                barrier, 1, device_id=(peer, me), device_id_type=pl.DeviceIdType.MESH
            )

    for c in range(size):
        part[c] = jnp.dot(
            context[...], wo[:, c * share : (c + 1) * share], preferred_element_type=jnp.float32
        ).astype(jnp.bfloat16)
    pl.semaphore_wait(barrier, expected)

    def spread(d):
        peer = lax.rem(me + d, size)
        return pltpu.make_async_remote_copy(
            part.at[peer], landed.at[d - 1], sum_send.at[d - 1], sum_recv.at[d - 1],
            device_id=(index, peer), device_id_type=pl.DeviceIdType.MESH,
        )

    def share_out(d):
        peer = lax.rem(me + d, size)
        return pltpu.make_async_remote_copy(
            full.at[me], full.at[me], all_send.at[d - 1], all_recv.at[d - 1],
            device_id=(index, peer), device_id_type=pl.DeviceIdType.MESH,
        )

    def share_in(d):
        source = lax.rem(me + size - d, size)
        return pltpu.make_async_remote_copy(
            full.at[source], full.at[source], all_send.at[d - 1], all_recv.at[d - 1],
            device_id=(index, source), device_id_type=pl.DeviceIdType.MESH,
        )

    for d in range(1, size):
        spread(d).start()
    total = part[me].astype(jnp.float32)
    for d in range(1, size):
        spread(d).wait_recv()
        total = total + landed[d - 1].astype(jnp.float32)
    full[me] = total.astype(jnp.bfloat16)
    for d in range(1, size):
        share_out(d).start()
    for d in range(1, size):
        share_in(d).wait_recv()

    square = jnp.zeros((hidden.shape[0], 1), jnp.float32)
    for c in range(size):
        residual = hidden[:, c * share : (c + 1) * share] + full[c].astype(jnp.float32)
        square = square + jnp.sum(residual * residual, axis=1, keepdims=True)
    factor = lax.rsqrt(square / hidden.shape[1] + EPSILON)
    answer = jnp.zeros(query.shape, jnp.float32)
    for c in range(size):
        columns = slice(c * share, (c + 1) * share)
        residual = hidden[:, columns] + full[c].astype(jnp.float32)
        normed = (residual * factor * gain[:, columns]).astype(jnp.bfloat16)
        answer = answer + jnp.dot(normed, wq[columns, :], preferred_element_type=jnp.float32)
    query[...] = answer.astype(jnp.bfloat16)

    def send_query(k):
        return pltpu.make_async_remote_copy(
            query, arrived.at[beam], out_send.at[k], out_recv.at[beam],
            device_id=(targets[k], me), device_id_type=pl.DeviceIdType.MESH,
        )

    for k in range(docs_here):

        @pl.when(targets[k] != index)
        def _(k=k):
            send_query(k).start()

        @pl.when(targets[k] == index)
        def _():
            arrived[beam] = query[...]

    for b in range(BEAMS):

        @pl.when(sources[b] != index)
        def _(b=b):
            pltpu.make_async_remote_copy(
                query, arrived.at[b], out_send.at[0], out_recv.at[b],
                device_id=(sources[b], me), device_id_type=pl.DeviceIdType.MESH,
            ).wait_recv()

    for d in range(1, size):
        spread(d).wait_send()
        share_out(d).wait_send()
    for k in range(docs_here):

        @pl.when(targets[k] != index)
        def _(k=k):
            send_query(k).wait_send()


def cross_queries(docs_here, context, wo, hidden, gain, wq):
    size = lax.axis_size("head")
    rows, features = hidden.shape
    share = features // size
    width = wq.shape[1]
    return pl.pallas_call(
        functools.partial(cross_query_kernel, docs_here),
        out_shape=jax.ShapeDtypeStruct((BEAMS, rows, width), jnp.bfloat16),
        in_specs=[pl.BlockSpec(memory_space=pltpu.VMEM)] * 5,
        out_specs=pl.BlockSpec(memory_space=pltpu.VMEM),
        scratch_shapes=[
            pltpu.VMEM((size, rows, share), jnp.bfloat16),
            pltpu.VMEM((size - 1, rows, share), jnp.bfloat16),
            pltpu.VMEM((size, rows, share), jnp.bfloat16),
            pltpu.VMEM((rows, width), jnp.bfloat16),
            pltpu.SemaphoreType.DMA((size - 1,)),
            pltpu.SemaphoreType.DMA((size - 1,)),
            pltpu.SemaphoreType.DMA((size - 1,)),
            pltpu.SemaphoreType.DMA((size - 1,)),
            pltpu.SemaphoreType.DMA((docs_here,)),
            pltpu.SemaphoreType.DMA((BEAMS,)),
        ],
        compiler_params=pltpu.CompilerParams(
            collective_id=0, has_side_effects=True, vmem_limit_bytes=32 * 1024 * 1024
        ),
        cost_estimate=pl.CostEstimate(
            flops=4 * rows * features * width, bytes_accessed=4 * features * width, transcendentals=0
        ),
    )(context, wo, hidden, gain.reshape(1, features), wq)


def shards(
    step_embeds,
    lang_table,
    lang_ids,
    self_gain,
    self_wq,
    self_wk,
    self_wv,
    self_wo,
    cross_gain,
    cross_wq,
    cross_wkv,
    encoder_rows,
    doc_lengths,
    past_keys,
    past_values,
    parents,
):
    hyp_count = lax.axis_size("hyp")
    group_size = hyp_count // BEAMS
    my_index = lax.axis_index("hyp")
    my_beam = my_index // group_size
    my_slot = my_index % group_size
    rows = step_embeds.shape[1]
    features = step_embeds.shape[2]
    head_width = self_wq.shape[1]
    heads = head_width // HEAD
    past = past_keys.shape[1]
    docs_here = lang_ids.shape[0] // group_size
    targets = lang_ids.shape[1]
    scaling = HEAD ** (-0.5)
    beam_groups = [[b * group_size + s for b in range(BEAMS)] for s in range(group_size)]

    cross_kv = project_rows(encoder_rows, cross_wkv)

    my_langs = lax.dynamic_slice_in_dim(lang_ids, my_slot * docs_here, docs_here, 0).reshape(rows)
    one_hot = (
        my_langs[:, None] == lax.broadcasted_iota(jnp.int32, (1, lang_table.shape[0]), 1)
    ).astype(jnp.bfloat16)
    lang_rows = jnp.dot(one_hot, lang_table, preferred_element_type=jnp.float32)
    hidden_in = (step_embeds.astype(jnp.float32) + lang_rows[None]).reshape(STEPS * rows, features)
    normed = rms_scaled(hidden_in, self_gain).astype(jnp.bfloat16)
    made = [
        jnp.dot(normed, w, preferred_element_type=jnp.float32).astype(jnp.bfloat16)
        for w in (self_wq, self_wk, self_wv)
    ]
    every = lax.all_gather(
        jnp.concatenate(made, axis=1), "hyp", axis=0, tiled=False, axis_index_groups=beam_groups
    ).reshape(BEAMS, STEPS, rows, 3, head_width)
    queries, keys, values = every[:, :, :, 0], every[:, :, :, 1], every[:, :, :, 2]

    parent_view = parents.reshape(STEPS, BEAMS, -1)
    moves = lax.dynamic_slice_in_dim(parent_view, my_slot * rows, rows, 2)
    ancestors = []
    for s in range(STEPS):
        chain = {s: None}
        current = moves[s]
        for j in range(s - 1, -2, -1):
            chain[j] = current
            if j >= 0:
                current = compose(moves[j], current)
        ancestors.append(chain)

    def of_mine(table):
        return lax.dynamic_index_in_dim(table, my_beam, 0, keepdims=False)

    past_k = past_keys.reshape(rows, past, heads, HEAD)
    past_v = past_values.reshape(rows, past, heads, HEAD)
    split_q = queries.reshape(BEAMS * STEPS, rows, heads, HEAD)
    scores = (
        jnp.einsum("nrhd,rphd->rhnp", split_q, past_k, preferred_element_type=jnp.float32)
        * scaling
    )
    highest = jnp.max(scores, axis=3)
    weights = jnp.exp(scores - highest[..., None])
    totals = jnp.sum(weights, axis=3)
    summed = jnp.einsum("rhnp,rphd->nrhd", weights, past_v.astype(jnp.float32))
    stats = jnp.stack([highest, totals], axis=-1).transpose(2, 0, 1, 3)
    packed = jnp.concatenate(
        [
            summed.reshape(BEAMS, STEPS * rows, head_width),
            stats.reshape(BEAMS, STEPS * rows, heads * 2),
        ],
        axis=2,
    )
    returned = lax.all_to_all(
        packed, "hyp", 0, 0, tiled=True, axis_index_groups=beam_groups
    ).reshape(BEAMS, STEPS, rows, head_width + heads * 2)
    past_of = jnp.stack([of_mine(ancestors[s][-1]) for s in range(STEPS)])
    chosen = pick([returned[b] for b in range(BEAMS)], past_of)
    part_sum = chosen[..., :head_width].reshape(STEPS, rows, heads, HEAD)
    part_stats = chosen[..., head_width:].reshape(STEPS, rows, heads, 2)

    contexts = []
    last_keys, last_values = [], []
    for s in range(STEPS):
        my_query = of_mine(queries[:, s]).reshape(rows, heads, HEAD).astype(jnp.float32)
        high, added, score_list, value_list = part_stats[s, ..., 0], None, [], []
        for j in range(s + 1):
            if j == s:
                key, value = of_mine(keys[:, j]), of_mine(values[:, j])
            else:
                owner = of_mine(ancestors[s][j])
                key = pick([keys[b, j] for b in range(BEAMS)], owner)
                value = pick([values[b, j] for b in range(BEAMS)], owner)
            if s == STEPS - 1:
                last_keys.append(key)
                last_values.append(value)
            key = key.reshape(rows, heads, HEAD).astype(jnp.float32)
            score_list.append(jnp.sum(my_query * key, axis=-1) * scaling)
            value_list.append(value.reshape(rows, heads, HEAD).astype(jnp.float32))
        top = high
        for score in score_list:
            top = jnp.maximum(top, score)
        factor = jnp.exp(high - top)
        total = part_stats[s, ..., 1] * factor
        context = part_sum[s] * factor[..., None]
        for score, value in zip(score_list, value_list):
            weight = jnp.exp(score - top)
            total = total + weight
            context = context + weight[..., None] * value
        contexts.append((context / total[..., None]).reshape(rows, head_width))
    self_context = jnp.concatenate(contexts, axis=0).astype(jnp.bfloat16)

    arrived = cross_queries(docs_here, self_context, self_wo, hidden_in, cross_gain, cross_wq)
    doc_queries = lax.dynamic_index_in_dim(
        arrived.reshape(BEAMS, STEPS, docs_here, targets, head_width),
        my_index % docs_here, 2, False,
    ).reshape(BEAMS * STEPS * targets, head_width)
    source_slot = my_index // docs_here
    slots = jnp.arange(group_size)
    answer = cross_attend(doc_queries, cross_kv, doc_lengths[0])

    by_beam = answer.reshape(BEAMS, 1, STEPS * targets, head_width)
    outgoing = jnp.where(
        (slots == source_slot)[None, :, None, None], by_beam, jnp.zeros((), by_beam.dtype)
    ).reshape(hyp_count, STEPS * targets, head_width)
    incoming = lax.all_to_all(outgoing, "hyp", 0, 0, tiled=True)
    mine = lax.dynamic_slice_in_dim(incoming, my_slot * docs_here, docs_here, 0)
    cross_context = (
        mine.reshape(docs_here, STEPS, targets, head_width)
        .transpose(1, 0, 2, 3)
        .reshape(STEPS, rows, head_width)
    )

    last = ancestors[STEPS - 1][-1]
    out_keys = final_cache(past_keys, 1, my_beam, last, group_size)
    out_values = final_cache(past_values, 2, my_beam, last, group_size)
    final_keys = jnp.concatenate([out_keys, jnp.stack(last_keys, axis=1)], axis=1)
    final_values = jnp.concatenate([out_values, jnp.stack(last_values, axis=1)], axis=1)
    return (cross_context, final_keys, final_values)


def solution(mesh):
    return jax.shard_map(
        shards,
        mesh=mesh,
        in_specs=(
            P(None, "hyp", None),
            P(),
            P(),
            P(),
            P(None, "head"),
            P(None, "head"),
            P(None, "head"),
            P("head", None),
            P(),
            P(None, "head"),
            P("hyp", "head"),
            P("hyp", "head"),
            P("hyp"),
            P("hyp", None, "head"),
            P("hyp", None, "head"),
            P(),
        ),
        out_specs=(P(None, "hyp", "head"), P("hyp", None, "head"), P("hyp", None, "head")),
        check_vma=False,
    )
```

```python
import functools

import jax
import jax.numpy as jnp
from jax import lax
from jax.experimental import pallas as pl
from jax.experimental.pallas import tpu as pltpu
from jax.sharding import PartitionSpec as P

HEAD = 256
BEAMS = 4
STEPS = 3
EPSILON = 1e-06


def rms_scaled(values_in, gain):
    mean_square = jnp.mean(values_in * values_in, axis=-1, keepdims=True)
    return values_in * lax.rsqrt(mean_square + EPSILON) * gain


def pick(candidates, selector):
    chosen = candidates[0]
    shape = selector.shape + (1,) * (chosen.ndim - selector.ndim)
    for position in range(1, len(candidates)):
        chosen = jnp.where((selector == position).reshape(shape), candidates[position], chosen)
    return chosen


def choose(flags, first, second):
    return jnp.where(flags.reshape(flags.shape + (1,) * (first.ndim - flags.ndim)), first, second)


def compose(outer, inner):
    return pick([jnp.broadcast_to(outer[b][None], inner.shape) for b in range(BEAMS)], inner)


def swap(block, bit, group_size):
    count = lax.axis_size("hyp")
    route = [(i, ((i // group_size) ^ bit) * group_size + i % group_size) for i in range(count)]
    return lax.ppermute(block, "hyp", route)


def final_cache(past, bit, my_beam, ancestors, group_size):
    other = 3 - bit
    mate = swap(past, bit, group_size)
    mine_set = (my_beam & bit) != 0
    low = jnp.where(mine_set, mate, past)
    high = jnp.where(mine_set, past, mate)
    peer_rows = lax.dynamic_index_in_dim(ancestors, my_beam ^ other, 0, keepdims=False)
    my_rows = lax.dynamic_index_in_dim(ancestors, my_beam, 0, keepdims=False)
    arrived = swap(choose((peer_rows & bit) != 0, high, low), other, group_size)
    local = choose((my_rows & bit) != 0, high, low)
    return choose((my_rows & other) == (my_beam & other), local, arrived)


def document_kernel(size, *refs):
    pieces, (weights, queries, length, out) = refs[: 2 * size - 1], refs[2 * size - 1 : 2 * size + 3]
    rows_all, weights_all, cross_kv, piece_sem, weight_sem = refs[2 * size + 3 :]
    me = lax.axis_index("head")
    width = pieces[0].shape[1]
    tiles = cross_kv.shape[0]

    def copy(position, owner):
        columns = pl.ds(pl.multiple_of(owner * width, width), width)
        return pltpu.make_async_copy(
            pieces[position], rows_all.at[:, columns], piece_sem.at[position]
        )

    def each(action):
        action(copy(0, me))
        for step in range(1, size):

            @pl.when(me >= step)
            def _():
                action(copy(step, me - step))

            @pl.when(me + step < size)
            def _():
                action(copy(size - 1 + step, me + step))

    whole = pltpu.make_async_copy(weights, weights_all, weight_sem)
    whole.start()
    each(lambda item: item.start())
    whole.wait()
    each(lambda item: item.wait())

    def project(tile, carry):
        columns = pl.ds(pl.multiple_of(tile * HEAD, HEAD), HEAD)
        cross_kv[tile] = jnp.dot(
            rows_all[...], weights_all[:, columns], preferred_element_type=jnp.float32
        ).astype(jnp.bfloat16)
        return carry

    lax.fori_loop(0, tiles, project, 0)
    live = lax.broadcasted_iota(jnp.int32, (1, cross_kv.shape[1]), 1) < length[0]
    for head in range(tiles // 2):
        columns = slice(head * HEAD, (head + 1) * HEAD)
        scores = lax.dot_general(
            queries[:, columns], cross_kv[2 * head], (((1,), (1,)), ((), ())),
            preferred_element_type=jnp.float32,
        ) * (HEAD ** (-0.5))
        scores = jnp.where(live, scores, -jnp.inf)
        raw_weights = jnp.exp(scores - jnp.max(scores, axis=1, keepdims=True))
        totals = jnp.sum(raw_weights, axis=1, keepdims=True)
        probs = (raw_weights / totals).astype(jnp.bfloat16)
        out[:, columns] = jnp.dot(
            probs, cross_kv[2 * head + 1], preferred_element_type=jnp.float32
        ).astype(jnp.bfloat16)


def document_attend(pieces, weights, queries, length):
    size = lax.axis_size("head")
    rows = pieces[0].shape[0]
    features, columns = weights.shape
    anywhere = pl.BlockSpec(memory_space=pl.ANY)
    return pl.pallas_call(
        functools.partial(document_kernel, size),
        out_shape=jax.ShapeDtypeStruct(queries.shape, jnp.bfloat16),
        in_specs=[anywhere] * (len(pieces) + 1)
        + [pl.BlockSpec(memory_space=pltpu.VMEM), pl.BlockSpec(memory_space=pltpu.SMEM)],
        out_specs=pl.BlockSpec(memory_space=pltpu.VMEM),
        scratch_shapes=[
            pltpu.VMEM((rows, features), jnp.bfloat16),
            pltpu.VMEM((features, columns), jnp.bfloat16),
            pltpu.VMEM((columns // HEAD, rows, HEAD), jnp.bfloat16),
            pltpu.SemaphoreType.DMA((len(pieces),)),
            pltpu.SemaphoreType.DMA,
        ],
        compiler_params=pltpu.CompilerParams(vmem_limit_bytes=40 * 1024 * 1024),
        cost_estimate=pl.CostEstimate(
            flops=2 * rows * features * columns,
            bytes_accessed=2 * features * (rows + columns),
            transcendentals=0,
        ),
    )(*pieces, weights, queries, length)


def travel(pair, step):
    size = lax.axis_size("head")
    up, down = pair
    upward = [(i, i + 1) for i in range(step - 1, size - 1)]
    downward = [(i + 1, i) for i in range(size - step)]
    return lax.ppermute(up, "head", upward), lax.ppermute(down, "head", downward)


def cross_query_kernel(
    docs_here, context, wo, hidden, gain, wq, arrived,
    part, landed, full, query, sum_send, sum_recv, all_send, all_recv, out_send, out_recv,
):
    size = lax.axis_size("head")
    me = lax.axis_index("head")
    hyps = lax.axis_size("hyp")
    group = hyps // BEAMS
    index = lax.axis_index("hyp")
    slot = lax.rem(index, group)
    beam = index // group
    share = part.shape[2]
    targets = [slot * docs_here + k for k in range(docs_here)]
    sources = [b * group + index // docs_here for b in range(BEAMS)]

    barrier = pltpu.get_barrier_semaphore()
    for d in range(1, size):
        pl.semaphore_signal(
            barrier, 1, device_id=(index, lax.rem(me + d, size)), device_id_type=pl.DeviceIdType.MESH
        )
    expected = jnp.int32(size - 1)
    for peer in targets + sources:
        expected = expected + (peer != index).astype(jnp.int32)

        @pl.when(peer != index)
        def _():
            pl.semaphore_signal(
                barrier, 1, device_id=(peer, me), device_id_type=pl.DeviceIdType.MESH
            )

    for c in range(size):
        part[c] = jnp.dot(
            context[...], wo[:, c * share : (c + 1) * share], preferred_element_type=jnp.float32
        ).astype(jnp.bfloat16)
    pl.semaphore_wait(barrier, expected)

    def spread(d):
        peer = lax.rem(me + d, size)
        return pltpu.make_async_remote_copy(
            part.at[peer], landed.at[d - 1], sum_send.at[d - 1], sum_recv.at[d - 1],
            device_id=(index, peer), device_id_type=pl.DeviceIdType.MESH,
        )

    def share_out(d):
        peer = lax.rem(me + d, size)
        return pltpu.make_async_remote_copy(
            full.at[me], full.at[me], all_send.at[d - 1], all_recv.at[d - 1],
            device_id=(index, peer), device_id_type=pl.DeviceIdType.MESH,
        )

    def share_in(d):
        source = lax.rem(me + size - d, size)
        return pltpu.make_async_remote_copy(
            full.at[source], full.at[source], all_send.at[d - 1], all_recv.at[d - 1],
            device_id=(index, source), device_id_type=pl.DeviceIdType.MESH,
        )

    for d in range(1, size):
        spread(d).start()
    total = part[me].astype(jnp.float32)
    for d in range(1, size):
        spread(d).wait_recv()
        total = total + landed[d - 1].astype(jnp.float32)
    full[me] = total.astype(jnp.bfloat16)
    for d in range(1, size):
        share_out(d).start()
    for d in range(1, size):
        share_in(d).wait_recv()

    square = jnp.zeros((hidden.shape[0], 1), jnp.float32)
    for c in range(size):
        residual = hidden[:, c * share : (c + 1) * share] + full[c].astype(jnp.float32)
        square = square + jnp.sum(residual * residual, axis=1, keepdims=True)
    factor = lax.rsqrt(square / hidden.shape[1] + EPSILON)
    answer = jnp.zeros(query.shape, jnp.float32)
    for c in range(size):
        columns = slice(c * share, (c + 1) * share)
        residual = hidden[:, columns] + full[c].astype(jnp.float32)
        normed = (residual * factor * gain[:, columns]).astype(jnp.bfloat16)
        answer = answer + jnp.dot(normed, wq[columns, :], preferred_element_type=jnp.float32)
    query[...] = answer.astype(jnp.bfloat16)

    def send_query(k):
        return pltpu.make_async_remote_copy(
            query, arrived.at[beam], out_send.at[k], out_recv.at[beam],
            device_id=(targets[k], me), device_id_type=pl.DeviceIdType.MESH,
        )

    for k in range(docs_here):

        @pl.when(targets[k] != index)
        def _(k=k):
            send_query(k).start()

        @pl.when(targets[k] == index)
        def _():
            arrived[beam] = query[...]

    for b in range(BEAMS):

        @pl.when(sources[b] != index)
        def _(b=b):
            pltpu.make_async_remote_copy(
                query, arrived.at[b], out_send.at[0], out_recv.at[b],
                device_id=(sources[b], me), device_id_type=pl.DeviceIdType.MESH,
            ).wait_recv()

    for d in range(1, size):
        spread(d).wait_send()
        share_out(d).wait_send()
    for k in range(docs_here):

        @pl.when(targets[k] != index)
        def _(k=k):
            send_query(k).wait_send()


def cross_queries(docs_here, context, wo, hidden, gain, wq):
    size = lax.axis_size("head")
    rows, features = hidden.shape
    share = features // size
    width = wq.shape[1]
    return pl.pallas_call(
        functools.partial(cross_query_kernel, docs_here),
        out_shape=jax.ShapeDtypeStruct((BEAMS, rows, width), jnp.bfloat16),
        in_specs=[pl.BlockSpec(memory_space=pltpu.VMEM)] * 5,
        out_specs=pl.BlockSpec(memory_space=pltpu.VMEM),
        scratch_shapes=[
            pltpu.VMEM((size, rows, share), jnp.bfloat16),
            pltpu.VMEM((size - 1, rows, share), jnp.bfloat16),
            pltpu.VMEM((size, rows, share), jnp.bfloat16),
            pltpu.VMEM((rows, width), jnp.bfloat16),
            pltpu.SemaphoreType.DMA((size - 1,)),
            pltpu.SemaphoreType.DMA((size - 1,)),
            pltpu.SemaphoreType.DMA((size - 1,)),
            pltpu.SemaphoreType.DMA((size - 1,)),
            pltpu.SemaphoreType.DMA((docs_here,)),
            pltpu.SemaphoreType.DMA((BEAMS,)),
        ],
        compiler_params=pltpu.CompilerParams(
            collective_id=0, has_side_effects=True, vmem_limit_bytes=32 * 1024 * 1024
        ),
        cost_estimate=pl.CostEstimate(
            flops=4 * rows * features * width,
            bytes_accessed=16 * features * width,
            transcendentals=0,
        ),
    )(context, wo, hidden, gain.reshape(1, features), wq)


def shards(
    step_embeds,
    lang_table,
    lang_ids,
    self_gain,
    self_wq,
    self_wk,
    self_wv,
    self_wo,
    cross_gain,
    cross_wq,
    cross_wkv,
    encoder_rows,
    doc_lengths,
    past_keys,
    past_values,
    parents,
):
    hyp_count = lax.axis_size("hyp")
    group_size = hyp_count // BEAMS
    my_index = lax.axis_index("hyp")
    my_beam = my_index // group_size
    my_slot = my_index % group_size
    rows = step_embeds.shape[1]
    features = step_embeds.shape[2]
    head_width = self_wq.shape[1]
    heads = head_width // HEAD
    past = past_keys.shape[1]
    docs_here = lang_ids.shape[0] // group_size
    targets = lang_ids.shape[1]
    scaling = HEAD ** (-0.5)
    beam_groups = [[b * group_size + s for b in range(BEAMS)] for s in range(group_size)]

    head_parts = lax.axis_size("head")
    full_weights = lax.all_gather(cross_wkv, "hyp", axis=0, tiled=True)
    hops = [travel((encoder_rows, encoder_rows), 1)]

    my_langs = lax.dynamic_slice_in_dim(lang_ids, my_slot * docs_here, docs_here, 0).reshape(rows)
    one_hot = (
        my_langs[:, None] == lax.broadcasted_iota(jnp.int32, (1, lang_table.shape[0]), 1)
    ).astype(jnp.bfloat16)
    lang_rows = jnp.dot(one_hot, lang_table, preferred_element_type=jnp.float32)
    hidden_in = (step_embeds.astype(jnp.float32) + lang_rows[None]).reshape(STEPS * rows, features)
    normed = rms_scaled(hidden_in, self_gain).astype(jnp.bfloat16)
    made = [
        jnp.dot(normed, w, preferred_element_type=jnp.float32).astype(jnp.bfloat16)
        for w in (self_wq, self_wk, self_wv)
    ]
    every = lax.all_gather(
        jnp.concatenate(made, axis=1), "hyp", axis=0, tiled=False, axis_index_groups=beam_groups
    )
    every, hops[0], late_keys, late_values = lax.optimization_barrier(
        (every, hops[0], past_keys, past_values)
    )
    every = every.reshape(BEAMS, STEPS, rows, 3, head_width)
    for step in range(2, max(head_parts - 1, 2)):
        hops.append(travel(hops[-1], step))
    queries, keys, values = every[:, :, :, 0], every[:, :, :, 1], every[:, :, :, 2]

    parent_view = parents.reshape(STEPS, BEAMS, -1)
    moves = lax.dynamic_slice_in_dim(parent_view, my_slot * rows, rows, 2)
    ancestors = []
    for s in range(STEPS):
        chain = {s: None}
        current = moves[s]
        for j in range(s - 1, -2, -1):
            chain[j] = current
            if j >= 0:
                current = compose(moves[j], current)
        ancestors.append(chain)

    def of_mine(table):
        return lax.dynamic_index_in_dim(table, my_beam, 0, keepdims=False)

    past_k = past_keys.reshape(rows, past, heads, HEAD)
    past_v = past_values.reshape(rows, past, heads, HEAD)
    split_q = queries.reshape(BEAMS * STEPS, rows, heads, HEAD)
    scores = (
        jnp.einsum("nrhd,rphd->rhnp", split_q, past_k, preferred_element_type=jnp.float32)
        * scaling
    )
    highest = jnp.max(scores, axis=3)
    weights = jnp.exp(scores - highest[..., None])
    totals = jnp.sum(weights, axis=3)
    summed = jnp.einsum("rhnp,rphd->nrhd", weights, past_v.astype(jnp.float32))
    stats = jnp.stack([highest, totals], axis=-1).transpose(2, 0, 1, 3)
    packed = jnp.concatenate(
        [
            summed.reshape(BEAMS, STEPS * rows, head_width),
            stats.reshape(BEAMS, STEPS * rows, heads * 2),
        ],
        axis=2,
    )
    returned = lax.all_to_all(
        packed, "hyp", 0, 0, tiled=True, axis_index_groups=beam_groups
    ).reshape(BEAMS, STEPS, rows, head_width + heads * 2)
    past_of = jnp.stack([of_mine(ancestors[s][-1]) for s in range(STEPS)])
    chosen = pick([returned[b] for b in range(BEAMS)], past_of)
    part_sum = chosen[..., :head_width].reshape(STEPS, rows, heads, HEAD)
    part_stats = chosen[..., head_width:].reshape(STEPS, rows, heads, 2)

    contexts = []
    last_keys, last_values = [], []
    for s in range(STEPS):
        my_query = of_mine(queries[:, s]).reshape(rows, heads, HEAD).astype(jnp.float32)
        high, added, score_list, value_list = part_stats[s, ..., 0], None, [], []
        for j in range(s + 1):
            if j == s:
                key, value = of_mine(keys[:, j]), of_mine(values[:, j])
            else:
                owner = of_mine(ancestors[s][j])
                key = pick([keys[b, j] for b in range(BEAMS)], owner)
                value = pick([values[b, j] for b in range(BEAMS)], owner)
            if s == STEPS - 1:
                last_keys.append(key)
                last_values.append(value)
            key = key.reshape(rows, heads, HEAD).astype(jnp.float32)
            score_list.append(jnp.sum(my_query * key, axis=-1) * scaling)
            value_list.append(value.reshape(rows, heads, HEAD).astype(jnp.float32))
        top = high
        for score in score_list:
            top = jnp.maximum(top, score)
        factor = jnp.exp(high - top)
        total = part_stats[s, ..., 1] * factor
        context = part_sum[s] * factor[..., None]
        for score, value in zip(score_list, value_list):
            weight = jnp.exp(score - top)
            total = total + weight
            context = context + weight[..., None] * value
        contexts.append((context / total[..., None]).reshape(rows, head_width))
    self_context = jnp.concatenate(contexts, axis=0).astype(jnp.bfloat16)

    self_context, hops[-1] = lax.optimization_barrier((self_context, hops[-1]))
    for step in range(len(hops) + 1, head_parts):
        hops.append(travel(hops[-1], step))
    arrived = cross_queries(docs_here, self_context, self_wo, hidden_in, cross_gain, cross_wq)
    doc_queries = lax.dynamic_index_in_dim(
        arrived.reshape(BEAMS, STEPS, docs_here, targets, head_width),
        my_index % docs_here, 2, False,
    ).reshape(BEAMS * STEPS * targets, head_width)
    source_slot = my_index // docs_here
    slots = jnp.arange(group_size)
    pieces = [encoder_rows] + [up for up, _ in hops] + [down for _, down in hops]
    answer = document_attend(pieces[: 2 * head_parts - 1], full_weights, doc_queries, doc_lengths)

    by_beam = answer.reshape(BEAMS, 1, STEPS * targets, head_width)
    outgoing = jnp.where(
        (slots == source_slot)[None, :, None, None], by_beam, jnp.zeros((), by_beam.dtype)
    ).reshape(hyp_count, STEPS * targets, head_width)
    incoming = lax.all_to_all(outgoing, "hyp", 0, 0, tiled=True)
    mine = lax.dynamic_slice_in_dim(incoming, my_slot * docs_here, docs_here, 0)
    cross_context = (
        mine.reshape(docs_here, STEPS, targets, head_width)
        .transpose(1, 0, 2, 3)
        .reshape(STEPS, rows, head_width)
    )

    last = ancestors[STEPS - 1][-1]
    out_keys = final_cache(late_keys, 1, my_beam, last, group_size)
    out_values = final_cache(late_values, 2, my_beam, last, group_size)
    final_keys = jnp.concatenate([out_keys, jnp.stack(last_keys, axis=1)], axis=1)
    final_values = jnp.concatenate([out_values, jnp.stack(last_values, axis=1)], axis=1)
    return (cross_context, final_keys, final_values)


def solution(mesh):
    return jax.shard_map(
        shards,
        mesh=mesh,
        in_specs=(
            P(None, "hyp", None),
            P(),
            P(),
            P(),
            P(None, "head"),
            P(None, "head"),
            P(None, "head"),
            P("head", None),
            P(),
            P(None, "head"),
            P("hyp", "head"),
            P("hyp", "head"),
            P("hyp"),
            P("hyp", None, "head"),
            P("hyp", None, "head"),
            P(),
        ),
        out_specs=(P(None, "hyp", "head"), P("hyp", None, "head"), P("hyp", None, "head")),
        check_vma=False,
    )
```

```python
import functools

import jax
import jax.numpy as jnp
from jax import lax
from jax.experimental import pallas as pl
from jax.experimental.pallas import tpu as pltpu
from jax.sharding import PartitionSpec as P

HEAD = 256
BEAMS = 4
STEPS = 3
EPSILON = 1e-06


def rms_scaled(values_in, gain):
    mean_square = jnp.mean(values_in * values_in, axis=-1, keepdims=True)
    return values_in * lax.rsqrt(mean_square + EPSILON) * gain


def pick(candidates, selector):
    chosen = candidates[0]
    shape = selector.shape + (1,) * (chosen.ndim - selector.ndim)
    for position in range(1, len(candidates)):
        chosen = jnp.where((selector == position).reshape(shape), candidates[position], chosen)
    return chosen


def choose(flags, first, second):
    return jnp.where(flags.reshape(flags.shape + (1,) * (first.ndim - flags.ndim)), first, second)


def compose(outer, inner):
    return pick([jnp.broadcast_to(outer[b][None], inner.shape) for b in range(BEAMS)], inner)


def swap(block, bit, group_size):
    count = lax.axis_size("hyp")
    route = [(i, ((i // group_size) ^ bit) * group_size + i % group_size) for i in range(count)]
    return lax.ppermute(block, "hyp", route)


def final_cache(past, bit, my_beam, ancestors, group_size):
    other = 3 - bit
    mate = swap(past, bit, group_size)
    mine_set = (my_beam & bit) != 0
    low = jnp.where(mine_set, mate, past)
    high = jnp.where(mine_set, past, mate)
    peer_rows = lax.dynamic_index_in_dim(ancestors, my_beam ^ other, 0, keepdims=False)
    my_rows = lax.dynamic_index_in_dim(ancestors, my_beam, 0, keepdims=False)
    arrived = swap(choose((peer_rows & bit) != 0, high, low), other, group_size)
    local = choose((my_rows & bit) != 0, high, low)
    return choose((my_rows & other) == (my_beam & other), local, arrived)


def document_kernel(size, *refs):
    pieces, (weights, queries, length, out) = refs[: 2 * size - 1], refs[2 * size - 1 : 2 * size + 3]
    rows_all, weights_all, cross_kv, piece_sem, weight_sem = refs[2 * size + 3 :]
    me = lax.axis_index("head")
    width = pieces[0].shape[1]
    tiles = cross_kv.shape[0]

    def copy(position, owner):
        columns = pl.ds(pl.multiple_of(owner * width, width), width)
        return pltpu.make_async_copy(
            pieces[position], rows_all.at[:, columns], piece_sem.at[position]
        )

    def each(action):
        action(copy(0, me))
        for step in range(1, size):

            @pl.when(me >= step)
            def _():
                action(copy(step, me - step))

            @pl.when(me + step < size)
            def _():
                action(copy(size - 1 + step, me + step))

    whole = pltpu.make_async_copy(weights, weights_all, weight_sem)
    whole.start()
    each(lambda item: item.start())
    whole.wait()
    each(lambda item: item.wait())

    def project(tile, carry):
        columns = pl.ds(pl.multiple_of(tile * HEAD, HEAD), HEAD)
        cross_kv[tile] = jnp.dot(
            rows_all[...], weights_all[:, columns], preferred_element_type=jnp.float32
        ).astype(jnp.bfloat16)
        return carry

    lax.fori_loop(0, tiles, project, 0)
    live = lax.broadcasted_iota(jnp.int32, (1, cross_kv.shape[1]), 1) < length[0]
    for head in range(tiles // 2):
        columns = slice(head * HEAD, (head + 1) * HEAD)
        scores = lax.dot_general(
            queries[:, columns], cross_kv[2 * head], (((1,), (1,)), ((), ())),
            preferred_element_type=jnp.float32,
        ) * (HEAD ** (-0.5))
        scores = jnp.where(live, scores, -jnp.inf)
        raw_weights = jnp.exp(scores - jnp.max(scores, axis=1, keepdims=True))
        totals = jnp.sum(raw_weights, axis=1, keepdims=True)
        probs = (raw_weights / totals).astype(jnp.bfloat16)
        out[:, columns] = jnp.dot(
            probs, cross_kv[2 * head + 1], preferred_element_type=jnp.float32
        ).astype(jnp.bfloat16)


def document_attend(pieces, weights, queries, length):
    size = lax.axis_size("head")
    rows = pieces[0].shape[0]
    features, columns = weights.shape
    anywhere = pl.BlockSpec(memory_space=pl.ANY)
    return pl.pallas_call(
        functools.partial(document_kernel, size),
        out_shape=jax.ShapeDtypeStruct(queries.shape, jnp.bfloat16),
        in_specs=[anywhere] * (len(pieces) + 1)
        + [pl.BlockSpec(memory_space=pltpu.VMEM), pl.BlockSpec(memory_space=pltpu.SMEM)],
        out_specs=pl.BlockSpec(memory_space=pltpu.VMEM),
        scratch_shapes=[
            pltpu.VMEM((rows, features), jnp.bfloat16),
            pltpu.VMEM((features, columns), jnp.bfloat16),
            pltpu.VMEM((columns // HEAD, rows, HEAD), jnp.bfloat16),
            pltpu.SemaphoreType.DMA((len(pieces),)),
            pltpu.SemaphoreType.DMA,
        ],
        compiler_params=pltpu.CompilerParams(vmem_limit_bytes=40 * 1024 * 1024),
        cost_estimate=pl.CostEstimate(
            flops=2 * rows * features * columns,
            bytes_accessed=2 * features * (rows + columns),
            transcendentals=0,
        ),
    )(*pieces, weights, queries, length)


def travel(pair, step):
    size = lax.axis_size("head")
    up, down = pair
    upward = [(i, i + 1) for i in range(step - 1, size - 1)]
    downward = [(i + 1, i) for i in range(size - step)]
    return lax.ppermute(up, "head", upward), lax.ppermute(down, "head", downward)


def cross_query_kernel(
    docs_here, context, wo, hidden, gain, wq, arrived,
    part, landed, full, query, sum_send, sum_recv, all_send, all_recv, out_send, out_recv,
):
    size = lax.axis_size("head")
    me = lax.axis_index("head")
    hyps = lax.axis_size("hyp")
    group = hyps // BEAMS
    index = lax.axis_index("hyp")
    slot = lax.rem(index, group)
    beam = index // group
    share = part.shape[2]
    targets = [slot * docs_here + k for k in range(docs_here)]
    sources = [b * group + index // docs_here for b in range(BEAMS)]

    barrier = pltpu.get_barrier_semaphore()
    for d in range(1, size):
        pl.semaphore_signal(
            barrier, 1, device_id=(index, lax.rem(me + d, size)), device_id_type=pl.DeviceIdType.MESH
        )
    expected = jnp.int32(size - 1)
    for peer in targets + sources:
        expected = expected + (peer != index).astype(jnp.int32)

        @pl.when(peer != index)
        def _():
            pl.semaphore_signal(
                barrier, 1, device_id=(peer, me), device_id_type=pl.DeviceIdType.MESH
            )

    for c in range(size):
        part[c] = jnp.dot(
            context[...], wo[:, c * share : (c + 1) * share], preferred_element_type=jnp.float32
        ).astype(jnp.bfloat16)
    pl.semaphore_wait(barrier, expected)

    def spread(d):
        peer = lax.rem(me + d, size)
        return pltpu.make_async_remote_copy(
            part.at[peer], landed.at[d - 1], sum_send.at[d - 1], sum_recv.at[d - 1],
            device_id=(index, peer), device_id_type=pl.DeviceIdType.MESH,
        )

    def share_out(d):
        peer = lax.rem(me + d, size)
        return pltpu.make_async_remote_copy(
            full.at[me], full.at[me], all_send.at[d - 1], all_recv.at[d - 1],
            device_id=(index, peer), device_id_type=pl.DeviceIdType.MESH,
        )

    def share_in(d):
        source = lax.rem(me + size - d, size)
        return pltpu.make_async_remote_copy(
            full.at[source], full.at[source], all_send.at[d - 1], all_recv.at[d - 1],
            device_id=(index, source), device_id_type=pl.DeviceIdType.MESH,
        )

    for d in range(1, size):
        spread(d).start()
    total = part[me].astype(jnp.float32)
    for d in range(1, size):
        spread(d).wait_recv()
        total = total + landed[d - 1].astype(jnp.float32)
    full[me] = total.astype(jnp.bfloat16)
    for d in range(1, size):
        share_out(d).start()
    for d in range(1, size):
        share_in(d).wait_recv()

    square = jnp.zeros((hidden.shape[0], 1), jnp.float32)
    for c in range(size):
        residual = hidden[:, c * share : (c + 1) * share] + full[c].astype(jnp.float32)
        square = square + jnp.sum(residual * residual, axis=1, keepdims=True)
    factor = lax.rsqrt(square / hidden.shape[1] + EPSILON)
    answer = jnp.zeros(query.shape, jnp.float32)
    for c in range(size):
        columns = slice(c * share, (c + 1) * share)
        residual = hidden[:, columns] + full[c].astype(jnp.float32)
        normed = (residual * factor * gain[:, columns]).astype(jnp.bfloat16)
        answer = answer + jnp.dot(normed, wq[columns, :], preferred_element_type=jnp.float32)
    query[...] = answer.astype(jnp.bfloat16)

    def send_query(k):
        return pltpu.make_async_remote_copy(
            query, arrived.at[beam], out_send.at[k], out_recv.at[beam],
            device_id=(targets[k], me), device_id_type=pl.DeviceIdType.MESH,
        )

    for k in range(docs_here):

        @pl.when(targets[k] != index)
        def _(k=k):
            send_query(k).start()

        @pl.when(targets[k] == index)
        def _():
            arrived[beam] = query[...]

    for b in range(BEAMS):

        @pl.when(sources[b] != index)
        def _(b=b):
            pltpu.make_async_remote_copy(
                query, arrived.at[b], out_send.at[0], out_recv.at[b],
                device_id=(sources[b], me), device_id_type=pl.DeviceIdType.MESH,
            ).wait_recv()

    for d in range(1, size):
        spread(d).wait_send()
        share_out(d).wait_send()
    for k in range(docs_here):

        @pl.when(targets[k] != index)
        def _(k=k):
            send_query(k).wait_send()


def cross_queries(docs_here, context, wo, hidden, gain, wq):
    size = lax.axis_size("head")
    rows, features = hidden.shape
    share = features // size
    width = wq.shape[1]
    return pl.pallas_call(
        functools.partial(cross_query_kernel, docs_here),
        out_shape=jax.ShapeDtypeStruct((BEAMS, rows, width), jnp.bfloat16),
        in_specs=[pl.BlockSpec(memory_space=pltpu.VMEM)] * 5,
        out_specs=pl.BlockSpec(memory_space=pltpu.VMEM),
        scratch_shapes=[
            pltpu.VMEM((size, rows, share), jnp.bfloat16),
            pltpu.VMEM((size - 1, rows, share), jnp.bfloat16),
            pltpu.VMEM((size, rows, share), jnp.bfloat16),
            pltpu.VMEM((rows, width), jnp.bfloat16),
            pltpu.SemaphoreType.DMA((size - 1,)),
            pltpu.SemaphoreType.DMA((size - 1,)),
            pltpu.SemaphoreType.DMA((size - 1,)),
            pltpu.SemaphoreType.DMA((size - 1,)),
            pltpu.SemaphoreType.DMA((docs_here,)),
            pltpu.SemaphoreType.DMA((BEAMS,)),
        ],
        compiler_params=pltpu.CompilerParams(
            collective_id=0, has_side_effects=True, vmem_limit_bytes=32 * 1024 * 1024
        ),
        cost_estimate=pl.CostEstimate(
            flops=4 * rows * features * width,
            bytes_accessed=16 * features * width,
            transcendentals=0,
        ),
    )(context, wo, hidden, gain.reshape(1, features), wq)


def shards(
    step_embeds,
    lang_table,
    lang_ids,
    self_gain,
    self_wq,
    self_wk,
    self_wv,
    self_wo,
    cross_gain,
    cross_wq,
    cross_wkv,
    encoder_rows,
    doc_lengths,
    past_keys,
    past_values,
    parents,
):
    hyp_count = lax.axis_size("hyp")
    group_size = hyp_count // BEAMS
    my_index = lax.axis_index("hyp")
    my_beam = my_index // group_size
    my_slot = my_index % group_size
    rows = step_embeds.shape[1]
    features = step_embeds.shape[2]
    head_width = self_wq.shape[1]
    heads = head_width // HEAD
    past = past_keys.shape[1]
    docs_here = lang_ids.shape[0] // group_size
    targets = lang_ids.shape[1]
    scaling = HEAD ** (-0.5)
    beam_groups = [[b * group_size + s for b in range(BEAMS)] for s in range(group_size)]

    head_parts = lax.axis_size("head")
    full_weights = lax.all_gather(cross_wkv, "hyp", axis=0, tiled=True)
    hops = [travel((encoder_rows, encoder_rows), 1)]

    my_langs = lax.dynamic_slice_in_dim(lang_ids, my_slot * docs_here, docs_here, 0).reshape(rows)
    one_hot = (
        my_langs[:, None] == lax.broadcasted_iota(jnp.int32, (1, lang_table.shape[0]), 1)
    ).astype(jnp.bfloat16)
    lang_rows = jnp.dot(one_hot, lang_table, preferred_element_type=jnp.float32)
    hidden_in = (step_embeds.astype(jnp.float32) + lang_rows[None]).reshape(STEPS * rows, features)
    normed = rms_scaled(hidden_in, self_gain).astype(jnp.bfloat16)
    made = [
        jnp.dot(normed, w, preferred_element_type=jnp.float32).astype(jnp.bfloat16)
        for w in (self_wq, self_wk, self_wv)
    ]
    every = lax.all_gather(
        jnp.concatenate(made, axis=1), "hyp", axis=0, tiled=False, axis_index_groups=beam_groups
    )
    every = every.reshape(BEAMS, STEPS, rows, 3, head_width)
    queries, keys, values = every[:, :, :, 0], every[:, :, :, 1], every[:, :, :, 2]

    parent_view = parents.reshape(STEPS, BEAMS, -1)
    moves = lax.dynamic_slice_in_dim(parent_view, my_slot * rows, rows, 2)
    ancestors = []
    for s in range(STEPS):
        chain = {s: None}
        current = moves[s]
        for j in range(s - 1, -2, -1):
            chain[j] = current
            if j >= 0:
                current = compose(moves[j], current)
        ancestors.append(chain)

    def of_mine(table):
        return lax.dynamic_index_in_dim(table, my_beam, 0, keepdims=False)

    past_k = past_keys.reshape(rows, past, heads, HEAD)
    past_v = past_values.reshape(rows, past, heads, HEAD)
    split_q = queries.reshape(BEAMS * STEPS, rows, heads, HEAD)
    scores = (
        jnp.einsum("nrhd,rphd->rhnp", split_q, past_k, preferred_element_type=jnp.float32)
        * scaling
    )
    highest = jnp.max(scores, axis=3)
    weights = jnp.exp(scores - highest[..., None])
    totals = jnp.sum(weights, axis=3)
    summed = jnp.einsum("rhnp,rphd->nrhd", weights, past_v.astype(jnp.float32))
    stats = jnp.stack([highest, totals], axis=-1).transpose(2, 0, 1, 3)
    packed = jnp.concatenate(
        [
            summed.reshape(BEAMS, STEPS * rows, head_width),
            stats.reshape(BEAMS, STEPS * rows, heads * 2),
        ],
        axis=2,
    )
    packed, hops[0], late_keys, late_values = lax.optimization_barrier(
        (packed, hops[0], past_keys, past_values)
    )
    for step in range(2, max(head_parts - 1, 2)):
        hops.append(travel(hops[-1], step))
    returned = lax.all_to_all(
        packed, "hyp", 0, 0, tiled=True, axis_index_groups=beam_groups
    ).reshape(BEAMS, STEPS, rows, head_width + heads * 2)
    past_of = jnp.stack([of_mine(ancestors[s][-1]) for s in range(STEPS)])
    chosen = pick([returned[b] for b in range(BEAMS)], past_of)
    part_sum = chosen[..., :head_width].reshape(STEPS, rows, heads, HEAD)
    part_stats = chosen[..., head_width:].reshape(STEPS, rows, heads, 2)

    contexts = []
    last_keys, last_values = [], []
    for s in range(STEPS):
        my_query = of_mine(queries[:, s]).reshape(rows, heads, HEAD).astype(jnp.float32)
        high, added, score_list, value_list = part_stats[s, ..., 0], None, [], []
        for j in range(s + 1):
            if j == s:
                key, value = of_mine(keys[:, j]), of_mine(values[:, j])
            else:
                owner = of_mine(ancestors[s][j])
                key = pick([keys[b, j] for b in range(BEAMS)], owner)
                value = pick([values[b, j] for b in range(BEAMS)], owner)
            if s == STEPS - 1:
                last_keys.append(key)
                last_values.append(value)
            key = key.reshape(rows, heads, HEAD).astype(jnp.float32)
            score_list.append(jnp.sum(my_query * key, axis=-1) * scaling)
            value_list.append(value.reshape(rows, heads, HEAD).astype(jnp.float32))
        top = high
        for score in score_list:
            top = jnp.maximum(top, score)
        factor = jnp.exp(high - top)
        total = part_stats[s, ..., 1] * factor
        context = part_sum[s] * factor[..., None]
        for score, value in zip(score_list, value_list):
            weight = jnp.exp(score - top)
            total = total + weight
            context = context + weight[..., None] * value
        contexts.append((context / total[..., None]).reshape(rows, head_width))
    self_context = jnp.concatenate(contexts, axis=0).astype(jnp.bfloat16)

    self_context, hops[-1] = lax.optimization_barrier((self_context, hops[-1]))
    for step in range(len(hops) + 1, head_parts):
        hops.append(travel(hops[-1], step))
    arrived = cross_queries(docs_here, self_context, self_wo, hidden_in, cross_gain, cross_wq)
    doc_queries = lax.dynamic_index_in_dim(
        arrived.reshape(BEAMS, STEPS, docs_here, targets, head_width),
        my_index % docs_here, 2, False,
    ).reshape(BEAMS * STEPS * targets, head_width)
    source_slot = my_index // docs_here
    slots = jnp.arange(group_size)
    pieces = [encoder_rows] + [up for up, _ in hops] + [down for _, down in hops]
    answer = document_attend(pieces[: 2 * head_parts - 1], full_weights, doc_queries, doc_lengths)

    by_beam = answer.reshape(BEAMS, 1, STEPS * targets, head_width)
    outgoing = jnp.where(
        (slots == source_slot)[None, :, None, None], by_beam, jnp.zeros((), by_beam.dtype)
    ).reshape(hyp_count, STEPS * targets, head_width)
    incoming = lax.all_to_all(outgoing, "hyp", 0, 0, tiled=True)
    mine = lax.dynamic_slice_in_dim(incoming, my_slot * docs_here, docs_here, 0)
    cross_context = (
        mine.reshape(docs_here, STEPS, targets, head_width)
        .transpose(1, 0, 2, 3)
        .reshape(STEPS, rows, head_width)
    )

    last = ancestors[STEPS - 1][-1]
    out_keys = final_cache(late_keys, 1, my_beam, last, group_size)
    out_values = final_cache(late_values, 2, my_beam, last, group_size)
    final_keys = jnp.concatenate([out_keys, jnp.stack(last_keys, axis=1)], axis=1)
    final_values = jnp.concatenate([out_values, jnp.stack(last_values, axis=1)], axis=1)
    return (cross_context, final_keys, final_values)


def solution(mesh):
    return jax.shard_map(
        shards,
        mesh=mesh,
        in_specs=(
            P(None, "hyp", None),
            P(),
            P(),
            P(),
            P(None, "head"),
            P(None, "head"),
            P(None, "head"),
            P("head", None),
            P(),
            P(None, "head"),
            P("hyp", "head"),
            P("hyp", "head"),
            P("hyp"),
            P("hyp", None, "head"),
            P("hyp", None, "head"),
            P(),
        ),
        out_specs=(P(None, "hyp", "head"), P("hyp", None, "head"), P("hyp", None, "head")),
        check_vma=False,
    )
```
